256 devices in a mesh: leaf: 64 (over z_lo, y, x), rhs: 4 (over z_hi, core).
Axes of the slice: x: 4, y: 4, z: 8 (z_hi: 2, z_lo: 4; z = z_hi * 4 + z_lo), core: 2. Of those that a mesh axis runs over, the one named last changes fastest.
Arguments:
- charges: bfloat16 [1024, 8, 2, 256], P('leaf'), may hold values from -6 to 6
- near_blocks: bfloat16 [1024, 4, 2, 256, 256], P('leaf', 'rhs'), may hold values from -0.125 to 0.125
- near_list: int32 [1024, 4], P('leaf', 'rhs'), may hold values from 0 to 1023, as said below
- basis: bfloat16 [1024, 2, 128, 256], P('leaf'), may hold values from -0.25 to 0.25
- coupling: bfloat16 [1024, 4, 2, 128, 128], P('leaf'), may hold values from -0.1875 to 0.1875
- coupling_list: int32 [1024, 4], P('leaf'), may hold values from 0 to 1023, as said below
- transfer: bfloat16 [1024, 2, 128, 128], P('leaf'), may hold values from -0.1875 to 0.1875
- top_coupling: bfloat16 [256, 4, 2, 128, 128], P('leaf'), may hold values from -0.1875 to 0.1875
- top_list: int32 [256, 4], P('leaf'), may hold values from 0 to 255
Outputs:
- product: bfloat16 [1024, 8, 2, 256], P('leaf', 'rhs')
The draws below stay inside these ranges and needn't reach their ends.
Inputs may be any that keep to these rules, and one draw needn't show every extreme that they name: `near_list`: every entry of row i lies within 16 leaves of i; entry 0 is i itself and entry 1 lies exactly 16 leaves from i. `coupling_list`: entry 0 of row i is (i + 512) modulo 1024; entry 1 lies exactly 16 leaves from i; every other entry lies 1 to 16 leaves from i.
All inputs are finite; a program needn't handle non-finite values.
Results may differ from the reference program's by a relative error of at most 0.0065.
Values may be sent and summed in bfloat16 or wider, within the bound.
No kernel may reach another device: no remote copies, remote signals or barrier semaphores. Data moves between devices by JAX's collectives and lax.ppermute only.
A program may use at most 64 MiB of HBM per device.

```python
import jax
import jax.numpy as jnp
from jax import lax

P_SIZE = 256
K = 128
KT = 128
NRHS = 8
NEAR = 4
CPL = 4
CPLT = 4
BR = 4
LEAF_DEV = 16
NLEAF = 1024
NTOP = 256


def draw_near_list(key, part):
    key = jax.random.fold_in(key, 11)
    row_index = jnp.arange(NLEAF, dtype=jnp.int32)[:, None]
    slot_index = jnp.arange(NEAR, dtype=jnp.int32)[None, :]
    offsets = jax.random.randint(key, (NLEAF, NEAR), -LEAF_DEV, LEAF_DEV + 1, dtype=jnp.int32)
    reach_offset = jnp.where(row_index >= LEAF_DEV, -LEAF_DEV, LEAF_DEV).astype(jnp.int32)
    offsets = jnp.where(slot_index == 0, 0, jnp.where(slot_index == 1, reach_offset, offsets))
    target = row_index + offsets
    target = jnp.where((target < 0) | (target >= NLEAF), row_index - offsets, target)
    return target.astype(jnp.int32)


def draw_coupling_list(key, part):
    key = jax.random.fold_in(key, 12)
    first_key, second_key = jax.random.split(key)
    row_index = jnp.arange(NLEAF, dtype=jnp.int32)[:, None]
    slot_index = jnp.arange(CPL, dtype=jnp.int32)[None, :]
    lengths_drawn = jax.random.randint(first_key, (NLEAF, CPL), 1, LEAF_DEV + 1, dtype=jnp.int32)
    sign_bits = jax.random.randint(second_key, (NLEAF, CPL), 0, 2, dtype=jnp.int32) * 2 - 1
    lengths_drawn = jnp.where(slot_index == 1, LEAF_DEV, lengths_drawn)
    offsets = lengths_drawn * sign_bits
    target = row_index + offsets
    target = jnp.where((target < 0) | (target >= NLEAF), row_index - offsets, target)
    distant = (row_index + NLEAF // 2) % NLEAF
    target = jnp.where(slot_index == 0, distant, target)
    return target.astype(jnp.int32)


def set_ends(drawn, rng, smallest, high):
    dims = drawn.shape
    index_at = [jax.random.randint(jax.random.fold_in(rng, axis), (), 0, dims[axis]) for axis in range(len(dims))]
    drawn = drawn.at[tuple(index_at)].set(smallest)
    longest = dims.index(max(dims))
    index_at[longest] = (index_at[longest] + 1) % dims[longest]
    return drawn.at[tuple(index_at)].set(high)


def level_of(key, shape, cuts, low, largest):
    level, own = 1.0, jax.random.fold_in(key, 6)
    for dim, parts in cuts:
        steps = jnp.exp(jax.random.uniform(jax.random.fold_in(own, dim), (parts,), jnp.float32, low / len(cuts), largest / len(cuts)))
        level = level * jnp.repeat(steps, shape[dim] // parts).reshape([-1 if axis == dim else 1 for axis in range(len(shape))])
    return level


def bell_draw(rng, dims, spread, reach, cuts=(), kind=jnp.bfloat16):
    result = spread * jax.random.normal(rng, dims, jnp.float32)
    if cuts:
        result = result * level_of(rng, dims, cuts, -0.22, 0.18)
    return jnp.clip(result, -reach, reach).astype(kind)


def setup_inputs(seed: int = 0) -> dict:
    splits = jax.random.split(jax.random.key(seed), 10)
    return {
        "charges": bell_draw(splits[0], (NLEAF, NRHS, 2, P_SIZE), 1.0, 6.0, ((0, 64),)),
        "near_blocks": bell_draw(splits[1], (NLEAF, NEAR, 2, P_SIZE, P_SIZE), (2 * P_SIZE * NEAR) ** -0.5, 0.125, ((0, 64), (1, 4))),
        "near_list": draw_near_list(jax.random.fold_in(splits[9], 71), 0),
        "basis": bell_draw(splits[3], (NLEAF, 2, K, P_SIZE), (2 * P_SIZE) ** -0.5, 0.25, ((0, 64),)),
        "coupling": bell_draw(splits[4], (NLEAF, CPL, 2, K, K), (2 * K * CPL) ** -0.5, 0.1875, ((0, 64),)),
        "coupling_list": draw_coupling_list(jax.random.fold_in(splits[9], 71), 0),
        "transfer": bell_draw(splits[6], (NLEAF, 2, K, KT), (2 * K * BR) ** -0.5, 0.1875, ((0, 64),)),
        "top_coupling": bell_draw(splits[7], (NTOP, CPLT, 2, KT, KT), (2 * KT * CPLT) ** -0.5, 0.1875, ((0, 64),)),
        "top_list": set_ends(jax.random.randint(splits[8], (NTOP, CPLT), 0, NTOP), jax.random.fold_in(splits[8], 1), 0, NTOP - 1).astype(jnp.int32),
    }


def combine(products):
    real_part = products[..., 0, 0, :] - products[..., 1, 1, :]
    imag_part = products[..., 0, 1, :] + products[..., 1, 0, :]
    return jnp.stack([real_part, imag_part], axis=-2)


def near_leaf(operands):
    blocks, sources = operands
    return combine(jnp.einsum("mapq,mrcq->racp", blocks.astype(jnp.float32), sources.astype(jnp.float32)))


def reference(charges, near_blocks, near_list, basis, coupling, coupling_list, transfer, top_coupling, top_list):
    coefficients = combine(jnp.einsum("lakp,lrcp->lrack", basis.astype(jnp.float32), charges.astype(jnp.float32))).astype(jnp.bfloat16)
    children = coefficients.reshape(NTOP, BR, NRHS, 2, K).astype(jnp.float32)
    grouped = transfer.reshape(NTOP, BR, 2, K, KT).astype(jnp.float32)
    parent_coef = combine(jnp.einsum("tbakq,tbrck->tracq", grouped, children)).astype(jnp.bfloat16)
    top_sources = jnp.take(parent_coef, top_list, axis=0).astype(jnp.float32)
    top_field = combine(jnp.einsum("tmaqs,tmrcs->tracq", top_coupling.astype(jnp.float32), top_sources)).astype(jnp.bfloat16)
    sources = jnp.take(coefficients, coupling_list, axis=0).astype(jnp.float32)
    leaf_field = combine(jnp.einsum("lmakj,lmrcj->lrack", coupling.astype(jnp.float32), sources))
    down_term = combine(jnp.einsum("tbakq,trcq->tbrack", grouped, top_field.astype(jnp.float32))).reshape(NLEAF, NRHS, 2, K)
    field_coef = (leaf_field + down_term).astype(jnp.bfloat16)
    far_part = combine(jnp.einsum("lakp,lrck->lracp", basis.astype(jnp.float32), field_coef.astype(jnp.float32)))
    near_sources = jnp.take(charges, near_list, axis=0)
    near_part = lax.map(near_leaf, (near_blocks, near_sources))
    return (far_part + near_part).astype(jnp.bfloat16)
```

```python
import jax
import jax.numpy as jnp
from jax import lax
from jax.sharding import PartitionSpec as P


def shifted(value, axis, step):
    count = lax.axis_size(axis)
    return lax.ppermute(value, axis, [(i, (i - step) % count) for i in range(count)])


def flipped(value, axis, bit):
    count = lax.axis_size(axis)
    return lax.ppermute(value, axis, [(i, i ^ bit) for i in range(count)])


def combine(products):
    real_part = products[..., 0, 0, :] - products[..., 1, 1, :]
    imag_part = products[..., 0, 1, :] + products[..., 1, 0, :]
    return jnp.stack([real_part, imag_part], axis=-2)


def local(
    charges,
    near_blocks,
    near_list,
    basis,
    coupling,
    coupling_list,
    transfer,
    top_coupling,
    top_list,
):
    leaves, rhs_all, _, points = charges.shape
    rhs_dev = rhs_all // lax.axis_size("rhs")
    top_dev = top_coupling.shape[0]
    branch = leaves // top_dev
    rank = basis.shape[2]
    top_rank = transfer.shape[3]
    groups = lax.axis_size("leaf")
    me = lax.axis_index("leaf")
    rhs = lax.axis_index("rhs")
    first_leaf = me * leaves
    own_rhs = lax.dynamic_slice_in_dim(charges, rhs * rhs_dev, rhs_dev, 1)
    coefficients = combine(
        jnp.einsum("lakp,lrcp->lrack", basis, own_rhs, preferred_element_type=jnp.float32)
    ).astype(jnp.bfloat16)
    grouped = transfer.reshape(top_dev, branch, 2, rank, top_rank)
    children = coefficients.reshape(top_dev, branch, rhs_dev, 2, rank)
    parent_coef = combine(
        jnp.einsum("tbakq,tbrck->tracq", grouped, children, preferred_element_type=jnp.float32)
    ).astype(jnp.bfloat16)

    flat_parent = parent_coef.reshape(-1, rank)
    flat_coef = coefficients.reshape(-1, rank)
    parent_rows, coef_rows = flat_parent.shape[0], flat_coef.shape[0]
    packed = jnp.concatenate([flat_parent, flat_coef, charges.reshape(-1, rank)], axis=0)
    low = shifted(packed, "leaf", -1)
    high = shifted(packed, "leaf", 1)
    table = jnp.stack(
        [low[:parent_rows], flat_parent, high[:parent_rows], shifted(flat_parent, "leaf", 2)]
    )
    ends = parent_rows + coef_rows
    charge_halo = jnp.concatenate(
        [low[ends:].reshape(charges.shape), charges, high[ends:].reshape(charges.shape)]
    )

    near_sources = jnp.take(charge_halo, near_list - first_leaf + leaves, axis=0)
    near_part = combine(
        jnp.einsum(
            "lmapq,lmrcq->lracp", near_blocks, near_sources, preferred_element_type=jnp.float32
        )
    )

    flat_table = table.reshape(-1, rank)
    far_pack = shifted(jnp.concatenate([flat_table, flat_coef], axis=0), "leaf", groups // 2)
    table = jnp.stack(
        [
            shifted(flat_table, "leaf", -16),
            flat_table,
            shifted(flat_table, "leaf", 16),
            far_pack[: flat_table.shape[0]],
        ]
    )
    table = jnp.stack([shifted(table, "leaf", -4), table, shifted(table, "leaf", 4), shifted(table, "leaf", 8)])

    halves = near_part.reshape(leaves, 2, rhs_all // 2, 2, points)
    half = rhs // 2
    mine = lax.dynamic_index_in_dim(halves, half, 1, False)
    other = lax.dynamic_index_in_dim(halves, 1 - half, 1, False)
    mine = mine + flipped(other.astype(jnp.bfloat16), "rhs", 2).astype(jnp.float32)
    quarters = mine.reshape(leaves, 2, rhs_dev, 2, points)
    core = rhs % 2
    mine = lax.dynamic_index_in_dim(quarters, core, 1, False)
    other = lax.dynamic_index_in_dim(quarters, 1 - core, 1, False)
    near_total = mine + flipped(other.astype(jnp.bfloat16), "rhs", 1).astype(jnp.float32)

    coef_shape = coefficients.shape
    coef_table = jnp.concatenate(
        [
            low[parent_rows:ends].reshape(coef_shape),
            coefficients,
            high[parent_rows:ends].reshape(coef_shape),
            far_pack[flat_table.shape[0] :].reshape(coef_shape),
        ]
    )
    near_place = coupling_list - first_leaf + leaves
    far_place = coupling_list - (first_leaf + groups // 2 * leaves) % (groups * leaves) + 3 * leaves
    distant = jnp.arange(coupling_list.shape[1])[None, :] == 0
    place = jnp.where(distant, far_place, near_place)
    sources = jnp.take(coef_table, place, axis=0)
    leaf_field = combine(
        jnp.einsum("lmakj,lmrcj->lrack", coupling, sources, preferred_element_type=jnp.float32)
    )

    turn = (top_list // top_dev - me + 21) % groups
    row = (((turn // 4) % 4 * 4 + turn // 16) * 4 + turn % 4) * top_dev + top_list % top_dev
    top_sources = jnp.take(table.reshape(-1, rhs_dev, 2, top_rank), row, axis=0)
    top_field = combine(
        jnp.einsum(
            "tmaqs,tmrcs->tracq", top_coupling, top_sources, preferred_element_type=jnp.float32
        )
    ).astype(jnp.bfloat16)
    down_term = combine(
        jnp.einsum("tbakq,trcq->tbrack", grouped, top_field, preferred_element_type=jnp.float32)
    ).reshape(leaves, rhs_dev, 2, rank)
    field_coef = (leaf_field + down_term).astype(jnp.bfloat16)
    far_part = combine(
        jnp.einsum("lakp,lrck->lracp", basis, field_coef, preferred_element_type=jnp.float32)
    )
    return (far_part + near_total).astype(jnp.bfloat16)


def solution(mesh):
    return jax.shard_map(
        local,
        mesh=mesh,
        in_specs=(
            P("leaf", None, None, None),
            P("leaf", "rhs", None, None, None),
            P("leaf", "rhs"),
            P("leaf", None, None, None),
            P("leaf", None, None, None, None),
            P("leaf", None),
            P("leaf", None, None, None),
            P("leaf", None, None, None, None),
            P("leaf", None),
        ),
        out_specs=P("leaf", "rhs", None, None),
        check_vma=False,
    )
```

```python
import functools

import jax
import jax.numpy as jnp
from jax import lax
from jax.experimental import pallas as pl
from jax.experimental.pallas import tpu as pltpu
from jax.sharding import PartitionSpec as P

F32 = jnp.float32
BF16 = jnp.bfloat16
ALONG_LAST = (((1,), (1,)), ((), ()))
ALONG_ROWS = (((1,), (0,)), ((), ()))


def dot(left, right, dims):
    return lax.dot_general(left, right, dims, preferred_element_type=F32)


def turned(value):
    rows = value.shape[0]
    even = lax.broadcasted_iota(jnp.int32, value.shape, 0) % 2 == 0
    return jnp.where(even, -pltpu.roll(value, rows - 1, 0), pltpu.roll(value, 1, 0))


def complex_rows(value):
    half = value.shape[1] // 2
    return value[:, :half] + turned(value[:, half:])


class Stream:
    def __init__(self, pairs, arrived, ahead):
        self.copies = [
            pltpu.make_async_copy(source, target, arrived.at[i])
            for i, (source, target) in enumerate(pairs)
        ]
        self.ahead = ahead
        for copy in self.copies[:ahead]:
            copy.start()

    def wait(self, index):
        self.copies[index].wait()
        if index + self.ahead < len(self.copies):
            self.copies[index + self.ahead].start()


def up_kernel(
    leaves, top_dev, own, charges_hbm, basis_hbm, transfer_hbm, parents, coefs, message,
    charges, basis, transfer, coef, rows, own_coef, own_parent, arrived,
):
    rank = basis.shape[2]
    branch = leaves // top_dev
    parts = [pl.ds(top * branch, branch) for top in range(top_dev)]
    stream = Stream(
        [(charges_hbm, charges)]
        + [(basis_hbm.at[part], basis.at[part]) for part in parts]
        + [(transfer_hbm.at[part], transfer.at[part]) for part in parts],
        arrived,
        1 + 2 * top_dev,
    )
    count = charges.shape[1] * 2
    first = pl.multiple_of(lax.axis_index("rhs") * own, own)
    coef_rows = leaves * own
    stream.wait(0)
    for leaf in range(leaves):
        if leaf % branch == 0:
            stream.wait(1 + leaf // branch)
        source = charges[leaf].reshape(count, charges.shape[3])
        product = dot(source, basis[leaf].reshape(2 * rank, -1), ALONG_LAST)
        coef[leaf] = complex_rows(product)
        own_coef[own * leaf : own * (leaf + 1), :] = coef[leaf, pl.ds(first, own), :]
        start = coef_rows + 2 * count * leaf
        message[start : start + count, :] = source[:, :rank]
        message[start + count : start + 2 * count, :] = source[:, rank:]
    coefs[...] = own_coef[...].astype(BF16)
    message[:coef_rows, :] = own_coef[...].astype(BF16)
    for top in range(top_dev):
        stream.wait(1 + top_dev + top)
        total = jnp.zeros((count, rank), F32)
        for leaf in range(top * branch, (top + 1) * branch):
            value = coef[leaf].astype(BF16).astype(F32)
            pair = jnp.concatenate([value, turned(value)], axis=1).astype(BF16)
            total += dot(pair, transfer[leaf].reshape(2 * rank, -1), ALONG_ROWS)
        rows[...] = total
        own_parent[own * top : own * (top + 1), :] = rows[pl.ds(first, own), :]
    parents[...] = jnp.broadcast_to(own_parent[...].astype(BF16)[None], parents.shape)


def near_kernel(
    leaves, own, near_hbm, places_hbm, message, even_side, odd_side, blocks_hbm, kept, sent, sources,
    near_list, places, blocks, table, coef_table, coef_wide, listed, tabled, arrived,
):
    points = blocks.shape[4]
    rank = message.shape[1]
    span = leaves * own
    size = message.shape[0] - span
    each = size // leaves
    count = each // 2
    lists = Stream([(near_hbm, near_list), (places_hbm, places)], listed, 2)
    me = lax.axis_index("leaf")
    order = ((even_side, 2 - 2 * (me % 2)), (message, 1), (odd_side, 2 * (me % 2)))
    tables = Stream(
        [
            (source.at[pl.ds(span, size)], table.at[pl.ds(pl.multiple_of(size * i, size), size)])
            for source, i in order
        ]
        + [
            (source.at[pl.ds(0, span)], coef_table.at[pl.ds(pl.multiple_of(span * i, span), span)])
            for source, i in order
        ],
        tabled,
        6,
    )
    step = 4
    chunks = [pl.ds(leaf, step) for leaf in range(0, leaves, step)]
    stream = Stream([(blocks_hbm.at[part], blocks.at[part]) for part in chunks], arrived, 4)
    first_leaf = me * leaves
    core = lax.axis_index("rhs") % 2
    for i in range(2):
        lists.wait(i)
    for i in range(6):
        tables.wait(i)
    others = []
    for leaf in range(leaves):
        place = (near_list[0, leaf] - first_leaf + leaves) * each
        value = table[pl.ds(pl.multiple_of(place, each), each), :]
        value = jnp.concatenate([value[:count], value[count:]], axis=1)
        if leaf % step == 0:
            stream.wait(leaf // step)
        product = dot(value, blocks[leaf, 0].reshape(2 * points, points), ALONG_LAST)
        value = complex_rows(product)
        for part in range(2):
            row = 2 * own * leaf + own * part
            first = value[2 * own * part : 2 * own * part + own]
            second = value[2 * own * part + own : 2 * own * (part + 1)]
            kept[row : row + own, :] = jnp.where(core == 0, first, second)
            others.append(jnp.where(core == 0, second, first))
    sent[...] = jnp.concatenate(others).astype(BF16)
    coef_wide[...] = coef_table[...].astype(F32)
    for leaf in range(leaves):
        for slot in range(1, places.shape[0]):
            place = pl.multiple_of((places[slot, leaf] - first_leaf + leaves) * own, own)
            sources[own * leaf : own * (leaf + 1), rank * (slot - 1) : rank * slot] = coef_wide[
                pl.ds(place, own), :
            ]


def coupling_kernel(leaves, own, distant, sources, coupling, field):
    rank = coupling.shape[4]
    for leaf in range(leaves):
        part = slice(own * leaf, own * (leaf + 1))
        value = jnp.concatenate([distant[part, :].astype(F32), sources[part, :]], axis=1)
        weights = jnp.concatenate(
            [coupling[leaf, slot].reshape(2 * rank, rank) for slot in range(coupling.shape[1])], axis=1
        )
        field[part, :] = complex_rows(dot(value.astype(BF16), weights, ALONG_LAST))


def sum_kernel(leaves, own, far, mine, received, product):
    for leaf in range(leaves):
        part = slice(own * leaf, own * (leaf + 1))
        value = far[part, :] + mine[part, :] + received[part, :].astype(F32)
        product[leaf] = value.astype(BF16).reshape(product.shape[1:])


def half_kernel(leaves, own, kept, received, mine, sent):
    part = lax.axis_index("rhs") // 2
    total = kept[...] + received[...].astype(F32)
    others = []
    for leaf in range(leaves):
        row = own * leaf
        first = total[2 * row : 2 * row + own]
        second = total[2 * row + own : 2 * row + 2 * own]
        mine[row : row + own, :] = jnp.where(part == 0, first, second)
        others.append(jnp.where(part == 0, second, first))
    sent[...] = jnp.concatenate(others).astype(BF16)


def down_kernel(
    leaves, own, tops_hbm, gathered, top_hbm, transfer, basis, field, result,
    tops, top_coupling, table, listed, arrived,
):
    rank = basis.shape[2]
    top_dev = top_coupling.shape[0]
    slots = top_coupling.shape[1]
    branch = leaves // top_dev
    lists = Stream([(tops_hbm, tops)], listed, 1)
    stream = Stream([(top_hbm.at[top], top_coupling.at[top]) for top in range(top_dev)], arrived, 4)
    table[...] = gathered[...].astype(F32).reshape(table.shape)
    lists.wait(0)
    for top in range(top_dev):
        values = []
        for slot in range(slots):
            values.append(table[pl.ds(pl.multiple_of(tops[top, slot] * own, own), own), :])
        value = jnp.concatenate(values, axis=1).astype(BF16)
        stream.wait(top)
        weights = jnp.concatenate(
            [top_coupling[top, slot].reshape(2 * rank, rank) for slot in range(slots)], axis=1
        )
        top_field = complex_rows(dot(value, weights, ALONG_LAST)).astype(BF16)
        for leaf in range(top * branch, (top + 1) * branch):
            down = complex_rows(dot(top_field, transfer[leaf].reshape(2 * rank, rank), ALONG_LAST))
            value = (down + field[own * leaf : own * (leaf + 1), :]).astype(BF16).astype(F32)
            pair = jnp.concatenate([value, turned(value)], axis=1).astype(BF16)
            result[own * leaf : own * (leaf + 1), :] = dot(
                pair, basis[leaf].reshape(2 * rank, -1), ALONG_ROWS
            )


VMEM = pl.BlockSpec(memory_space=pltpu.VMEM)
SMEM = pl.BlockSpec(memory_space=pltpu.SMEM)
HBM = pl.BlockSpec(memory_space=pltpu.HBM)
ANY = pl.BlockSpec(memory_space=pl.ANY)


def call(kernel, out_shape, scratch, ops, specs, flops, room):
    ops = [
        pltpu.with_memory_space_constraint(value, pltpu.HBM) if specs.get(i) is HBM else value
        for i, value in enumerate(ops)
    ]
    return pl.pallas_call(
        kernel,
        out_shape=[jax.ShapeDtypeStruct(*shape) for shape in out_shape],
        in_specs=[specs.get(i, VMEM) for i in range(len(ops))],
        out_specs=[VMEM] * len(out_shape),
        scratch_shapes=scratch,
        compiler_params=pltpu.CompilerParams(vmem_limit_bytes=room * 2**20),
        cost_estimate=pl.CostEstimate(flops=flops, bytes_accessed=4 * 2**20, transcendentals=0),
    )(*ops)


def shifted(value, axis, step):
    count = lax.axis_size(axis)
    return lax.ppermute(value, axis, [(i, (i - step) % count) for i in range(count)])


def paired(value, axis, first):
    count = lax.axis_size(axis)
    pairs = []
    for i in range(first, count - 1, 2):
        pairs += [(i, i + 1), (i + 1, i)]
    return lax.ppermute(value, axis, pairs)


def flipped(value, axis, bit):
    count = lax.axis_size(axis)
    return lax.ppermute(value, axis, [(i, i ^ bit) for i in range(count)])


def local(
    charges,
    near_blocks,
    near_list,
    basis,
    coupling,
    coupling_list,
    transfer,
    top_coupling,
    top_list,
):
    leaves, rhs_all, _, points = charges.shape
    rhs_dev = rhs_all // lax.axis_size("rhs")
    top_dev = top_coupling.shape[0]
    rank = basis.shape[2]
    groups = lax.axis_size("leaf")
    count, own = 2 * rhs_all, 2 * rhs_dev
    parent_rows, coef_rows = top_dev * own, leaves * own
    parents, coefs, message = call(
        functools.partial(up_kernel, leaves, top_dev, own),
        [
            ((groups, parent_rows, rank), BF16),
            ((coef_rows, rank), BF16),
            ((coef_rows + leaves * 2 * count, rank), BF16),
        ],
        [
            pltpu.VMEM(charges.shape, BF16),
            pltpu.VMEM(basis.shape, BF16),
            pltpu.VMEM(transfer.shape, BF16),
            pltpu.VMEM((leaves, count, rank), F32),
            pltpu.VMEM((count, rank), F32),
            pltpu.VMEM((coef_rows, rank), F32),
            pltpu.VMEM((parent_rows, rank), F32),
            pltpu.SemaphoreType.DMA((1 + 2 * top_dev,)),
        ],
        (charges, basis, transfer),
        {0: HBM, 1: HBM, 2: HBM},
        2 * 10**8,
        8,
    )
    gathered = lax.all_to_all(parents, "leaf", 0, 0, tiled=True)
    odd_side = paired(message, "leaf", 1)
    even_side = paired(message, "leaf", 0)
    distant = shifted(coefs, "leaf", groups // 2)
    kept, sent, sources = call(
        functools.partial(near_kernel, leaves, own),
        [
            ((leaves * 2 * own, points), F32),
            ((leaves * 2 * own, points), BF16),
            ((coef_rows, 3 * rank), F32),
        ],
        [
            pltpu.SMEM((1, leaves), jnp.int32),
            pltpu.SMEM((coupling_list.shape[1], leaves), jnp.int32),
            pltpu.VMEM(near_blocks.shape, BF16),
            pltpu.VMEM((3 * leaves * 2 * count, rank), BF16),
            pltpu.VMEM((3 * coef_rows, rank), BF16),
            pltpu.VMEM((3 * coef_rows, rank), F32),
            pltpu.SemaphoreType.DMA((2,)),
            pltpu.SemaphoreType.DMA((6,)),
            pltpu.SemaphoreType.DMA((leaves // 4,)),
        ],
        (near_list.T, coupling_list.T, message, even_side, odd_side, near_blocks),
        {0: HBM, 1: HBM, 2: ANY, 3: ANY, 4: ANY, 5: HBM},
        2 * 10**9,
        8,
    )
    received = flipped(sent, "rhs", 1)
    (field,) = call(
        functools.partial(coupling_kernel, leaves, own),
        [((coef_rows, rank), F32)],
        [],
        (distant, sources, coupling),
        {},
        2 * 10**9,
        6,
    )
    mine, sent = call(
        functools.partial(half_kernel, leaves, own),
        [((leaves * own, points), F32), ((leaves * own, points), BF16)],
        [],
        (kept, received),
        {},
        10**7,
        2,
    )
    received = flipped(sent, "rhs", 2)
    (far_part,) = call(
        functools.partial(down_kernel, leaves, own),
        [((leaves * own, points), F32)],
        [
            pltpu.SMEM(top_list.shape, jnp.int32),
            pltpu.VMEM(top_coupling.shape, BF16),
            pltpu.VMEM((groups * parent_rows, rank), F32),
            pltpu.SemaphoreType.DMA((1,)),
            pltpu.SemaphoreType.DMA((top_dev,)),
        ],
        (top_list, gathered, top_coupling, transfer, basis, field),
        {0: HBM, 2: HBM},
        2 * 10**9,
        6,
    )
    (product,) = call(
        functools.partial(sum_kernel, leaves, own),
        [((leaves, rhs_dev, 2, points), BF16)],
        [],
        (far_part, mine, received),
        {},
        10**7,
        2,
    )
    return product


def solution(mesh):
    return jax.shard_map(
        local,
        mesh=mesh,
        in_specs=(
            P("leaf", None, None, None),
            P("leaf", "rhs", None, None, None),
            P("leaf", "rhs"),
            P("leaf", None, None, None),
            P("leaf", None, None, None, None),
            P("leaf", None),
            P("leaf", None, None, None),
            P("leaf", None, None, None, None),
            P("leaf", None),
        ),
        out_specs=P("leaf", "rhs", None, None),
        check_vma=False,
    )
```

```python
import functools

import jax
import jax.numpy as jnp
from jax import lax
from jax.experimental import pallas as pl
from jax.experimental.pallas import tpu as pltpu
from jax.sharding import PartitionSpec as P

F32 = jnp.float32
BF16 = jnp.bfloat16
ALONG_LAST = (((1,), (1,)), ((), ()))
ALONG_ROWS = (((1,), (0,)), ((), ()))


def dot(left, right, dims):
    return lax.dot_general(left, right, dims, preferred_element_type=F32)


def turned(value):
    rows = value.shape[0]
    even = lax.broadcasted_iota(jnp.int32, value.shape, 0) % 2 == 0
    return jnp.where(even, -pltpu.roll(value, rows - 1, 0), pltpu.roll(value, 1, 0))


def complex_rows(value):
    half = value.shape[1] // 2
    return value[:, :half] + turned(value[:, half:])


class Stream:
    def __init__(self, pairs, arrived, ahead):
        self.copies = [
            pltpu.make_async_copy(source, target, arrived.at[i])
            for i, (source, target) in enumerate(pairs)
        ]
        self.ahead = ahead
        for copy in self.copies[:ahead]:
            copy.start()

    def wait(self, index):
        self.copies[index].wait()
        if index + self.ahead < len(self.copies):
            self.copies[index + self.ahead].start()


def up_kernel(
    leaves, top_dev, own, charges_hbm, basis_hbm, transfer_hbm, parents, coefs, message,
    charges, basis, transfer, held, coef, rows, own_coef, own_parent, arrived,
):
    rank = basis.shape[2]
    branch = leaves // top_dev
    parts = [pl.ds(top * branch, branch) for top in range(top_dev)]
    stream = Stream(
        [(charges_hbm, charges)]
        + [(basis_hbm.at[part], basis.at[part]) for part in parts]
        + [(transfer_hbm.at[part], transfer.at[part]) for part in parts],
        arrived,
        1 + 2 * top_dev,
    )
    count = charges.shape[1] * 2
    first = pl.multiple_of(lax.axis_index("rhs") * own, own)
    coef_rows = leaves * own
    stream.wait(0)
    for leaf in range(leaves):
        source = charges[leaf].reshape(count, charges.shape[3])
        held[leaf] = source
        start = coef_rows + 2 * count * leaf
        message[start : start + count, :] = source[:, :rank]
        message[start + count : start + 2 * count, :] = source[:, rank:]
    for leaf in range(leaves):
        if leaf % (2 * branch) == 0:
            stream.wait(1 + leaf // branch)
            stream.wait(2 + leaf // branch)
        product = dot(held[leaf], basis[leaf].reshape(2 * rank, -1), ALONG_LAST)
        coef[leaf] = complex_rows(product)
    for leaf in range(leaves):
        own_coef[own * leaf : own * (leaf + 1), :] = coef[leaf, pl.ds(first, own), :]
    coefs[...] = own_coef[...].astype(BF16)
    message[:coef_rows, :] = own_coef[...].astype(BF16)
    for top in range(top_dev):
        stream.wait(1 + top_dev + top)
    for top in range(top_dev):
        total = jnp.zeros((count, rank), F32)
        for leaf in range(top * branch, (top + 1) * branch):
            value = coef[leaf].astype(BF16).astype(F32)
            pair = jnp.concatenate([value, turned(value)], axis=1).astype(BF16)
            total += dot(pair, transfer[leaf].reshape(2 * rank, -1), ALONG_ROWS)
        rows[...] = total
        own_parent[own * top : own * (top + 1), :] = rows[pl.ds(first, own), :]
    parents[...] = jnp.broadcast_to(own_parent[...].astype(BF16)[None], parents.shape)


def near_kernel(
    leaves, own, near_hbm, places_hbm, message, even_side, odd_side, blocks_hbm, kept, sent, sources,
    near_list, places, blocks, table, held, coef_table, coef_wide, listed, tabled, arrived,
):
    points = blocks.shape[4]
    rank = message.shape[1]
    span = leaves * own
    size = message.shape[0] - span
    each = size // leaves
    count = each // 2
    lists = Stream([(near_hbm, near_list), (places_hbm, places)], listed, 2)
    me = lax.axis_index("leaf")
    order = ((even_side, 2 - 2 * (me % 2)), (message, 1), (odd_side, 2 * (me % 2)))
    tables = Stream(
        [
            (source.at[pl.ds(span, size)], table.at[pl.ds(pl.multiple_of(size * i, size), size)])
            for source, i in order
        ]
        + [
            (source.at[pl.ds(0, span)], coef_table.at[pl.ds(pl.multiple_of(span * i, span), span)])
            for source, i in order
        ],
        tabled,
        6,
    )
    step = 4
    chunks = [pl.ds(leaf, step) for leaf in range(0, leaves, step)]
    stream = Stream([(blocks_hbm.at[part], blocks.at[part]) for part in chunks], arrived, 4)
    first_leaf = me * leaves
    core = lax.axis_index("rhs") % 2
    for i in range(2):
        lists.wait(i)
    for i in range(6):
        tables.wait(i)
    for leaf in range(leaves):
        place = (near_list[0, leaf] - first_leaf + leaves) * each
        value = table[pl.ds(pl.multiple_of(place, each), each), :]
        held[leaf] = jnp.concatenate([value[:count], value[count:]], axis=1)
    coef_wide[...] = coef_table[...].astype(F32)
    for leaf in range(leaves):
        for slot in range(1, places.shape[0]):
            place = pl.multiple_of((places[slot, leaf] - first_leaf + leaves) * own, own)
            sources[own * leaf : own * (leaf + 1), rank * (slot - 1) : rank * slot] = coef_wide[
                pl.ds(place, own), :
            ]
    others = []
    for leaf in range(leaves):
        if leaf % step == 0:
            stream.wait(leaf // step)
        product = dot(held[leaf], blocks[leaf, 0].reshape(2 * points, points), ALONG_LAST)
        value = complex_rows(product)
        for part in range(2):
            row = 2 * own * leaf + own * part
            first = value[2 * own * part : 2 * own * part + own]
            second = value[2 * own * part + own : 2 * own * (part + 1)]
            kept[row : row + own, :] = jnp.where(core == 0, first, second)
            others.append(jnp.where(core == 0, second, first))
    sent[...] = jnp.concatenate(others).astype(BF16)


def coupling_kernel(leaves, own, distant, sources, coupling, field):
    rank = coupling.shape[4]
    for leaf in range(leaves):
        part = slice(own * leaf, own * (leaf + 1))
        value = jnp.concatenate([distant[part, :].astype(F32), sources[part, :]], axis=1)
        weights = jnp.concatenate(
            [coupling[leaf, slot].reshape(2 * rank, rank) for slot in range(coupling.shape[1])], axis=1
        )
        field[part, :] = complex_rows(dot(value.astype(BF16), weights, ALONG_LAST))


def sum_kernel(leaves, own, far, mine, received, product):
    for leaf in range(leaves):
        part = slice(own * leaf, own * (leaf + 1))
        value = far[part, :] + mine[part, :] + received[part, :].astype(F32)
        product[leaf] = value.astype(BF16).reshape(product.shape[1:])


def half_kernel(leaves, own, kept, received, mine, sent):
    part = lax.axis_index("rhs") // 2
    total = kept[...] + received[...].astype(F32)
    others = []
    for leaf in range(leaves):
        row = own * leaf
        first = total[2 * row : 2 * row + own]
        second = total[2 * row + own : 2 * row + 2 * own]
        mine[row : row + own, :] = jnp.where(part == 0, first, second)
        others.append(jnp.where(part == 0, second, first))
    sent[...] = jnp.concatenate(others).astype(BF16)


def down_kernel(
    leaves, own, tops_hbm, gathered, top_coupling, transfer, basis_hbm, field, result,
    tops, basis, table, listed, arrived,
):
    rank = transfer.shape[2]
    top_dev = top_coupling.shape[0]
    slots = top_coupling.shape[1]
    branch = leaves // top_dev
    lists = Stream([(tops_hbm, tops)], listed, 1)
    stream = Stream([(basis_hbm, basis)], arrived, 1)
    table[...] = gathered[...].astype(F32).reshape(table.shape)
    lists.wait(0)
    pairs = []
    for top in range(top_dev):
        values = []
        for slot in range(slots):
            values.append(table[pl.ds(pl.multiple_of(tops[top, slot] * own, own), own), :])
        value = jnp.concatenate(values, axis=1).astype(BF16)
        weights = jnp.concatenate(
            [top_coupling[top, slot].reshape(2 * rank, rank) for slot in range(slots)], axis=1
        )
        top_field = complex_rows(dot(value, weights, ALONG_LAST)).astype(BF16)
        for leaf in range(top * branch, (top + 1) * branch):
            down = complex_rows(dot(top_field, transfer[leaf].reshape(2 * rank, rank), ALONG_LAST))
            value = (down + field[own * leaf : own * (leaf + 1), :]).astype(BF16).astype(F32)
            pairs.append(jnp.concatenate([value, turned(value)], axis=1).astype(BF16))
    stream.wait(0)
    for leaf in range(leaves):
        result[own * leaf : own * (leaf + 1), :] = dot(
            pairs[leaf], basis[leaf].reshape(2 * rank, -1), ALONG_ROWS
        )


VMEM = pl.BlockSpec(memory_space=pltpu.VMEM)
SMEM = pl.BlockSpec(memory_space=pltpu.SMEM)
HBM = pl.BlockSpec(memory_space=pltpu.HBM)
ANY = pl.BlockSpec(memory_space=pl.ANY)


def call(kernel, out_shape, scratch, ops, specs, flops, room):
    ops = [
        pltpu.with_memory_space_constraint(value, pltpu.HBM) if specs.get(i) is HBM else value
        for i, value in enumerate(ops)
    ]
    return pl.pallas_call(
        kernel,
        out_shape=[jax.ShapeDtypeStruct(*shape) for shape in out_shape],
        in_specs=[specs.get(i, VMEM) for i in range(len(ops))],
        out_specs=[VMEM] * len(out_shape),
        scratch_shapes=scratch,
        compiler_params=pltpu.CompilerParams(vmem_limit_bytes=room * 2**20),
        cost_estimate=pl.CostEstimate(flops=flops, bytes_accessed=4 * 2**20, transcendentals=0),
    )(*ops)


def shifted(value, axis, step):
    count = lax.axis_size(axis)
    return lax.ppermute(value, axis, [(i, (i - step) % count) for i in range(count)])


def paired(value, axis, first):
    count = lax.axis_size(axis)
    pairs = []
    for i in range(first, count - 1, 2):
        pairs += [(i, i + 1), (i + 1, i)]
    return lax.ppermute(value, axis, pairs)


def flipped(value, axis, bit):
    count = lax.axis_size(axis)
    return lax.ppermute(value, axis, [(i, i ^ bit) for i in range(count)])


def local(
    charges,
    near_blocks,
    near_list,
    basis,
    coupling,
    coupling_list,
    transfer,
    top_coupling,
    top_list,
):
    leaves, rhs_all, _, points = charges.shape
    rhs_dev = rhs_all // lax.axis_size("rhs")
    top_dev = top_coupling.shape[0]
    rank = basis.shape[2]
    groups = lax.axis_size("leaf")
    count, own = 2 * rhs_all, 2 * rhs_dev
    parent_rows, coef_rows = top_dev * own, leaves * own
    parents, coefs, message = call(
        functools.partial(up_kernel, leaves, top_dev, own),
        [
            ((groups, parent_rows, rank), BF16),
            ((coef_rows, rank), BF16),
            ((coef_rows + leaves * 2 * count, rank), BF16),
        ],
        [
            pltpu.VMEM(charges.shape, BF16),
            pltpu.VMEM(basis.shape, BF16),
            pltpu.VMEM(transfer.shape, BF16),
            pltpu.VMEM((leaves, count, points), BF16),
            pltpu.VMEM((leaves, count, rank), F32),
            pltpu.VMEM((count, rank), F32),
            pltpu.VMEM((coef_rows, rank), F32),
            pltpu.VMEM((parent_rows, rank), F32),
            pltpu.SemaphoreType.DMA((1 + 2 * top_dev,)),
        ],
        (charges, basis, transfer),
        {0: HBM, 1: HBM, 2: HBM},
        2 * 10**8,
        8,
    )
    gathered = lax.all_to_all(parents, "leaf", 0, 0, tiled=True)
    odd_side = paired(message, "leaf", 1)
    even_side = paired(message, "leaf", 0)
    distant = shifted(coefs, "leaf", groups // 2)
    kept, sent, sources = call(
        functools.partial(near_kernel, leaves, own),
        [
            ((leaves * 2 * own, points), F32),
            ((leaves * 2 * own, points), BF16),
            ((coef_rows, 3 * rank), F32),
        ],
        [
            pltpu.SMEM((1, leaves), jnp.int32),
            pltpu.SMEM((coupling_list.shape[1], leaves), jnp.int32),
            pltpu.VMEM(near_blocks.shape, BF16),
            pltpu.VMEM((3 * leaves * 2 * count, rank), BF16),
            pltpu.VMEM((leaves, count, points), BF16),
            pltpu.VMEM((3 * coef_rows, rank), BF16),
            pltpu.VMEM((3 * coef_rows, rank), F32),
            pltpu.SemaphoreType.DMA((2,)),
            pltpu.SemaphoreType.DMA((6,)),
            pltpu.SemaphoreType.DMA((leaves // 4,)),
        ],
        (near_list.T, coupling_list.T, message, even_side, odd_side, near_blocks),
        {0: HBM, 1: HBM, 2: ANY, 3: ANY, 4: ANY, 5: HBM},
        2 * 10**9,
        8,
    )
    received = flipped(sent, "rhs", 1)
    mine, sent = call(
        functools.partial(half_kernel, leaves, own),
        [((leaves * own, points), F32), ((leaves * own, points), BF16)],
        [],
        (kept, received),
        {},
        2 * 10**9,
        2,
    )
    sources, mine = lax.optimization_barrier((sources, mine))
    received = flipped(sent, "rhs", 2)
    (field,) = call(
        functools.partial(coupling_kernel, leaves, own),
        [((coef_rows, rank), F32)],
        [],
        (distant, sources, coupling),
        {},
        2 * 10**9,
        6,
    )
    (far_part,) = call(
        functools.partial(down_kernel, leaves, own),
        [((leaves * own, points), F32)],
        [
            pltpu.SMEM(top_list.shape, jnp.int32),
            pltpu.VMEM(basis.shape, BF16),
            pltpu.VMEM((groups * parent_rows, rank), F32),
            pltpu.SemaphoreType.DMA((1,)),
            pltpu.SemaphoreType.DMA((1,)),
        ],
        (top_list, gathered, top_coupling, transfer, basis, field),
        {0: HBM, 4: HBM},
        2 * 10**9,
        6,
    )
    (product,) = call(
        functools.partial(sum_kernel, leaves, own),
        [((leaves, rhs_dev, 2, points), BF16)],
        [],
        (far_part, mine, received),
        {},
        10**7,
        2,
    )
    return product


def solution(mesh):
    return jax.shard_map(
        local,
        mesh=mesh,
        in_specs=(
            P("leaf", None, None, None),
            P("leaf", "rhs", None, None, None),
            P("leaf", "rhs"),
            P("leaf", None, None, None),
            P("leaf", None, None, None, None),
            P("leaf", None),
            P("leaf", None, None, None),
            P("leaf", None, None, None, None),
            P("leaf", None),
        ),
        out_specs=P("leaf", "rhs", None, None),
        check_vma=False,
    )
```

```python
import functools

import jax
import jax.numpy as jnp
from jax import lax
from jax.experimental import pallas as pl
from jax.experimental.pallas import tpu as pltpu
from jax.sharding import PartitionSpec as P

F32 = jnp.float32
BF16 = jnp.bfloat16
ALONG_LAST = (((1,), (1,)), ((), ()))
ALONG_ROWS = (((1,), (0,)), ((), ()))


def dot(left, right, dims):
    return lax.dot_general(left, right, dims, preferred_element_type=F32)


def turned(value):
    rows = value.shape[0]
    even = lax.broadcasted_iota(jnp.int32, value.shape, 0) % 2 == 0
    return jnp.where(even, -pltpu.roll(value, rows - 1, 0), pltpu.roll(value, 1, 0))


def complex_rows(value):
    half = value.shape[1] // 2
    return value[:, :half] + turned(value[:, half:])


class Stream:
    def __init__(self, pairs, arrived, ahead):
        self.copies = [
            pltpu.make_async_copy(source, target, arrived.at[i])
            for i, (source, target) in enumerate(pairs)
        ]
        self.ahead = ahead
        for copy in self.copies[:ahead]:
            copy.start()

    def wait(self, index):
        self.copies[index].wait()
        if index + self.ahead < len(self.copies):
            self.copies[index + self.ahead].start()


def up_kernel(
    leaves, top_dev, own, charges_hbm, basis_hbm, transfer_hbm, blocks_hbm, parents, coefs, message, early,
    charges, basis, transfer, held, coef, rows, own_coef, own_parent, arrived,
):
    rank = basis.shape[2]
    branch = leaves // top_dev
    parts = [pl.ds(top * branch, branch) for top in range(top_dev)]
    stream = Stream(
        [(charges_hbm, charges)]
        + [(basis_hbm.at[part], basis.at[part]) for part in parts]
        + [(transfer_hbm.at[part], transfer.at[part]) for part in parts]
        + [(blocks_hbm.at[pl.ds(0, early.shape[0])], early)],
        arrived,
        2 + 2 * top_dev,
    )
    count = charges.shape[1] * 2
    first = pl.multiple_of(lax.axis_index("rhs") * own, own)
    coef_rows = leaves * own
    stream.wait(0)
    for leaf in range(leaves):
        source = charges[leaf].reshape(count, charges.shape[3])
        held[leaf] = source
        start = coef_rows + 2 * count * leaf
        message[start : start + count, :] = source[:, :rank]
        message[start + count : start + 2 * count, :] = source[:, rank:]
    for leaf in range(leaves):
        if leaf % (2 * branch) == 0:
            stream.wait(1 + leaf // branch)
            stream.wait(2 + leaf // branch)
        product = dot(held[leaf], basis[leaf].reshape(2 * rank, -1), ALONG_LAST)
        coef[leaf] = complex_rows(product)
    for leaf in range(leaves):
        own_coef[own * leaf : own * (leaf + 1), :] = coef[leaf, pl.ds(first, own), :]
    coefs[...] = own_coef[...].astype(BF16)
    message[:coef_rows, :] = own_coef[...].astype(BF16)
    for top in range(top_dev):
        stream.wait(1 + top_dev + top)
    for top in range(top_dev):
        total = jnp.zeros((count, rank), F32)
        for leaf in range(top * branch, (top + 1) * branch):
            value = coef[leaf].astype(BF16).astype(F32)
            pair = jnp.concatenate([value, turned(value)], axis=1).astype(BF16)
            total += dot(pair, transfer[leaf].reshape(2 * rank, -1), ALONG_ROWS)
        rows[...] = total
        own_parent[own * top : own * (top + 1), :] = rows[pl.ds(first, own), :]
    stream.wait(1 + 2 * top_dev)
    parents[...] = jnp.broadcast_to(own_parent[...].astype(BF16)[None], parents.shape)


def near_kernel(
    leaves, own, near_hbm, places_hbm, message, even_side, odd_side, early, blocks_hbm, kept, sent, sources,
    near_list, places, blocks, table, held, coef_table, coef_wide, listed, tabled, arrived,
):
    points = blocks.shape[4]
    rank = message.shape[1]
    span = leaves * own
    size = message.shape[0] - span
    each = size // leaves
    count = each // 2
    lists = Stream([(near_hbm, near_list), (places_hbm, places)], listed, 2)
    me = lax.axis_index("leaf")
    order = ((even_side, 2 - 2 * (me % 2)), (message, 1), (odd_side, 2 * (me % 2)))
    tables = Stream(
        [
            (source.at[pl.ds(span, size)], table.at[pl.ds(pl.multiple_of(size * i, size), size)])
            for source, i in order
        ]
        + [
            (source.at[pl.ds(0, span)], coef_table.at[pl.ds(pl.multiple_of(span * i, span), span)])
            for source, i in order
        ],
        tabled,
        6,
    )
    step = 4
    begin = early.shape[0]
    stream = Stream(
        [
            (blocks_hbm.at[pl.ds(leaf, step)], blocks.at[pl.ds(leaf - begin, step)])
            for leaf in range(begin, leaves, step)
        ],
        arrived,
        4,
    )
    first_leaf = me * leaves
    core = lax.axis_index("rhs") % 2
    for i in range(2):
        lists.wait(i)
    for i in range(6):
        tables.wait(i)
    for leaf in range(leaves):
        place = (near_list[0, leaf] - first_leaf + leaves) * each
        value = table[pl.ds(pl.multiple_of(place, each), each), :]
        held[leaf] = jnp.concatenate([value[:count], value[count:]], axis=1)
    coef_wide[...] = coef_table[...].astype(F32)
    for leaf in range(leaves):
        for slot in range(1, places.shape[0]):
            place = pl.multiple_of((places[slot, leaf] - first_leaf + leaves) * own, own)
            sources[own * leaf : own * (leaf + 1), rank * (slot - 1) : rank * slot] = coef_wide[
                pl.ds(place, own), :
            ]
    others = []
    for leaf in range(leaves):
        if leaf >= begin and leaf % step == 0:
            stream.wait((leaf - begin) // step)
        block = early[leaf, 0] if leaf < begin else blocks[leaf - begin, 0]
        product = dot(held[leaf], block.reshape(2 * points, points), ALONG_LAST)
        value = complex_rows(product)
        for part in range(2):
            row = 2 * own * leaf + own * part
            first = value[2 * own * part : 2 * own * part + own]
            second = value[2 * own * part + own : 2 * own * (part + 1)]
            kept[row : row + own, :] = jnp.where(core == 0, first, second)
            others.append(jnp.where(core == 0, second, first))
    sent[...] = jnp.concatenate(others).astype(BF16)


def coupling_kernel(leaves, own, distant, sources, coupling, field):
    rank = coupling.shape[4]
    for leaf in range(leaves):
        part = slice(own * leaf, own * (leaf + 1))
        value = jnp.concatenate([distant[part, :].astype(F32), sources[part, :]], axis=1)
        weights = jnp.concatenate(
            [coupling[leaf, slot].reshape(2 * rank, rank) for slot in range(coupling.shape[1])], axis=1
        )
        field[part, :] = complex_rows(dot(value.astype(BF16), weights, ALONG_LAST))


def sum_kernel(leaves, own, far, mine, received, product):
    for leaf in range(leaves):
        part = slice(own * leaf, own * (leaf + 1))
        value = far[part, :] + mine[part, :] + received[part, :].astype(F32)
        product[leaf] = value.astype(BF16).reshape(product.shape[1:])


def half_kernel(leaves, own, kept, received, mine, sent):
    part = lax.axis_index("rhs") // 2
    total = kept[...] + received[...].astype(F32)
    others = []
    for leaf in range(leaves):
        row = own * leaf
        first = total[2 * row : 2 * row + own]
        second = total[2 * row + own : 2 * row + 2 * own]
        mine[row : row + own, :] = jnp.where(part == 0, first, second)
        others.append(jnp.where(part == 0, second, first))
    sent[...] = jnp.concatenate(others).astype(BF16)


def down_kernel(
    leaves, own, tops_hbm, gathered, top_coupling, transfer, basis_hbm, field, result,
    tops, basis, table, listed, arrived,
):
    rank = transfer.shape[2]
    top_dev = top_coupling.shape[0]
    slots = top_coupling.shape[1]
    branch = leaves // top_dev
    lists = Stream([(tops_hbm, tops)], listed, 1)
    stream = Stream([(basis_hbm, basis)], arrived, 1)
    table[...] = gathered[...].astype(F32).reshape(table.shape)
    lists.wait(0)
    pairs = []
    for top in range(top_dev):
        values = []
        for slot in range(slots):
            values.append(table[pl.ds(pl.multiple_of(tops[top, slot] * own, own), own), :])
        value = jnp.concatenate(values, axis=1).astype(BF16)
        weights = jnp.concatenate(
            [top_coupling[top, slot].reshape(2 * rank, rank) for slot in range(slots)], axis=1
        )
        top_field = complex_rows(dot(value, weights, ALONG_LAST)).astype(BF16)
        for leaf in range(top * branch, (top + 1) * branch):
            down = complex_rows(dot(top_field, transfer[leaf].reshape(2 * rank, rank), ALONG_LAST))
            value = (down + field[own * leaf : own * (leaf + 1), :]).astype(BF16).astype(F32)
            pairs.append(jnp.concatenate([value, turned(value)], axis=1).astype(BF16))
    stream.wait(0)
    for leaf in range(leaves):
        result[own * leaf : own * (leaf + 1), :] = dot(
            pairs[leaf], basis[leaf].reshape(2 * rank, -1), ALONG_ROWS
        )


VMEM = pl.BlockSpec(memory_space=pltpu.VMEM)
SMEM = pl.BlockSpec(memory_space=pltpu.SMEM)
HBM = pl.BlockSpec(memory_space=pltpu.HBM)
ANY = pl.BlockSpec(memory_space=pl.ANY)


def call(kernel, out_shape, scratch, ops, specs, flops, room):
    ops = [
        pltpu.with_memory_space_constraint(value, pltpu.HBM) if specs.get(i) is HBM else value
        for i, value in enumerate(ops)
    ]
    return pl.pallas_call(
        kernel,
        out_shape=[jax.ShapeDtypeStruct(*shape) for shape in out_shape],
        in_specs=[specs.get(i, VMEM) for i in range(len(ops))],
        out_specs=[VMEM] * len(out_shape),
        scratch_shapes=scratch,
        compiler_params=pltpu.CompilerParams(vmem_limit_bytes=room * 2**20),
        cost_estimate=pl.CostEstimate(flops=flops, bytes_accessed=4 * 2**20, transcendentals=0),
    )(*ops)


def shifted(value, axis, step):
    count = lax.axis_size(axis)
    return lax.ppermute(value, axis, [(i, (i - step) % count) for i in range(count)])


def paired(value, axis, first):
    count = lax.axis_size(axis)
    pairs = []
    for i in range(first, count - 1, 2):
        pairs += [(i, i + 1), (i + 1, i)]
    return lax.ppermute(value, axis, pairs)


def flipped(value, axis, bit):
    count = lax.axis_size(axis)
    return lax.ppermute(value, axis, [(i, i ^ bit) for i in range(count)])


def local(
    charges,
    near_blocks,
    near_list,
    basis,
    coupling,
    coupling_list,
    transfer,
    top_coupling,
    top_list,
):
    leaves, rhs_all, _, points = charges.shape
    rhs_dev = rhs_all // lax.axis_size("rhs")
    top_dev = top_coupling.shape[0]
    rank = basis.shape[2]
    groups = lax.axis_size("leaf")
    count, own = 2 * rhs_all, 2 * rhs_dev
    parent_rows, coef_rows = top_dev * own, leaves * own
    parents, coefs, message, early = call(
        functools.partial(up_kernel, leaves, top_dev, own),
        [
            ((groups, parent_rows, rank), BF16),
            ((coef_rows, rank), BF16),
            ((coef_rows + leaves * 2 * count, rank), BF16),
            ((leaves // 2, *near_blocks.shape[1:]), BF16),
        ],
        [
            pltpu.VMEM(charges.shape, BF16),
            pltpu.VMEM(basis.shape, BF16),
            pltpu.VMEM(transfer.shape, BF16),
            pltpu.VMEM((leaves, count, points), BF16),
            pltpu.VMEM((leaves, count, rank), F32),
            pltpu.VMEM((count, rank), F32),
            pltpu.VMEM((coef_rows, rank), F32),
            pltpu.VMEM((parent_rows, rank), F32),
            pltpu.SemaphoreType.DMA((2 + 2 * top_dev,)),
        ],
        (charges, basis, transfer, near_blocks),
        {0: HBM, 1: HBM, 2: HBM, 3: HBM},
        2 * 10**8,
        12,
    )
    gathered = lax.all_to_all(parents, "leaf", 0, 0, tiled=True)
    odd_side = paired(message, "leaf", 1)
    even_side = paired(message, "leaf", 0)
    distant = shifted(coefs, "leaf", groups // 2)
    kept, sent, sources = call(
        functools.partial(near_kernel, leaves, own),
        [
            ((leaves * 2 * own, points), F32),
            ((leaves * 2 * own, points), BF16),
            ((coef_rows, 3 * rank), F32),
        ],
        [
            pltpu.SMEM((1, leaves), jnp.int32),
            pltpu.SMEM((coupling_list.shape[1], leaves), jnp.int32),
            pltpu.VMEM((leaves // 2, *near_blocks.shape[1:]), BF16),
            pltpu.VMEM((3 * leaves * 2 * count, rank), BF16),
            pltpu.VMEM((leaves, count, points), BF16),
            pltpu.VMEM((3 * coef_rows, rank), BF16),
            pltpu.VMEM((3 * coef_rows, rank), F32),
            pltpu.SemaphoreType.DMA((2,)),
            pltpu.SemaphoreType.DMA((6,)),
            pltpu.SemaphoreType.DMA((leaves // 8,)),
        ],
        (near_list.T, coupling_list.T, message, even_side, odd_side, early, near_blocks),
        {0: HBM, 1: HBM, 2: ANY, 3: ANY, 4: ANY, 6: HBM},
        2 * 10**9,
        8,
    )
    received = flipped(sent, "rhs", 1)
    mine, sent = call(
        functools.partial(half_kernel, leaves, own),
        [((leaves * own, points), F32), ((leaves * own, points), BF16)],
        [],
        (kept, received),
        {},
        2 * 10**9,
        2,
    )
    sources, mine = lax.optimization_barrier((sources, mine))
    received = flipped(sent, "rhs", 2)
    (field,) = call(
        functools.partial(coupling_kernel, leaves, own),
        [((coef_rows, rank), F32)],
        [],
        (distant, sources, coupling),
        {},
        2 * 10**9,
        6,
    )
    (far_part,) = call(
        functools.partial(down_kernel, leaves, own),
        [((leaves * own, points), F32)],
        [
            pltpu.SMEM(top_list.shape, jnp.int32),
            pltpu.VMEM(basis.shape, BF16),
            pltpu.VMEM((groups * parent_rows, rank), F32),
            pltpu.SemaphoreType.DMA((1,)),
            pltpu.SemaphoreType.DMA((1,)),
        ],
        (top_list, gathered, top_coupling, transfer, basis, field),
        {0: HBM, 4: HBM},
        2 * 10**9,
        6,
    )
    (product,) = call(
        functools.partial(sum_kernel, leaves, own),
        [((leaves, rhs_dev, 2, points), BF16)],
        [],
        (far_part, mine, received),
        {},
        10**7,
        2,
    )
    return product


def solution(mesh):
    return jax.shard_map(
        local,
        mesh=mesh,
        in_specs=(
            P("leaf", None, None, None),
            P("leaf", "rhs", None, None, None),
            P("leaf", "rhs"),
            P("leaf", None, None, None),
            P("leaf", None, None, None, None),
            P("leaf", None),
            P("leaf", None, None, None),
            P("leaf", None, None, None, None),
            P("leaf", None),
        ),
        out_specs=P("leaf", "rhs", None, None),
        check_vma=False,
    )
```

```python
import functools

import jax
import jax.numpy as jnp
from jax import lax
from jax.experimental import pallas as pl
from jax.experimental.pallas import tpu as pltpu
from jax.sharding import PartitionSpec as P

F32 = jnp.float32
BF16 = jnp.bfloat16
ALONG_LAST = (((1,), (1,)), ((), ()))
ALONG_ROWS = (((1,), (0,)), ((), ()))


def dot(left, right, dims):
    return lax.dot_general(left, right, dims, preferred_element_type=F32)


def turned(value):
    rows = value.shape[0]
    even = lax.broadcasted_iota(jnp.int32, value.shape, 0) % 2 == 0
    return jnp.where(even, -pltpu.roll(value, rows - 1, 0), pltpu.roll(value, 1, 0))


def complex_rows(value):
    half = value.shape[1] // 2
    return value[:, :half] + turned(value[:, half:])


class Stream:
    def __init__(self, pairs, arrived, ahead):
        self.copies = [
            pltpu.make_async_copy(source, target, arrived.at[i])
            for i, (source, target) in enumerate(pairs)
        ]
        self.ahead = ahead
        for copy in self.copies[:ahead]:
            copy.start()

    def wait(self, index):
        self.copies[index].wait()
        if index + self.ahead < len(self.copies):
            self.copies[index + self.ahead].start()


def up_kernel(
    leaves, top_dev, own, charges_hbm, basis_hbm, transfer_hbm, blocks_hbm, parents, coefs, message, early,
    charges, basis, transfer, held, coef, rows, own_coef, own_parent, arrived,
):
    rank = basis.shape[2]
    branch = leaves // top_dev
    parts = [pl.ds(top * branch, branch) for top in range(top_dev)]
    stream = Stream(
        [(charges_hbm, charges)]
        + [(basis_hbm.at[part], basis.at[part]) for part in parts]
        + [(transfer_hbm.at[part], transfer.at[part]) for part in parts]
        + [(blocks_hbm.at[pl.ds(0, early.shape[0])], early)],
        arrived,
        2 + 2 * top_dev,
    )
    count = charges.shape[1] * 2
    first = pl.multiple_of(lax.axis_index("rhs") * own, own)
    coef_rows = leaves * own
    stream.wait(0)
    for leaf in range(leaves):
        source = charges[leaf].reshape(count, charges.shape[3])
        held[leaf] = source
        start = coef_rows + 2 * count * leaf
        message[start : start + count, :] = source[:, :rank]
        message[start + count : start + 2 * count, :] = source[:, rank:]
    for leaf in range(leaves):
        if leaf % (2 * branch) == 0:
            stream.wait(1 + leaf // branch)
            stream.wait(2 + leaf // branch)
        product = dot(held[leaf], basis[leaf].reshape(2 * rank, -1), ALONG_LAST)
        coef[leaf] = complex_rows(product)
    for leaf in range(leaves):
        own_coef[own * leaf : own * (leaf + 1), :] = coef[leaf, pl.ds(first, own), :]
    coefs[...] = own_coef[...].astype(BF16)
    message[:coef_rows, :] = own_coef[...].astype(BF16)
    for top in range(top_dev):
        stream.wait(1 + top_dev + top)
    for top in range(top_dev):
        total = jnp.zeros((count, rank), F32)
        for leaf in range(top * branch, (top + 1) * branch):
            value = coef[leaf].astype(BF16).astype(F32)
            pair = jnp.concatenate([value, turned(value)], axis=1).astype(BF16)
            total += dot(pair, transfer[leaf].reshape(2 * rank, -1), ALONG_ROWS)
        rows[...] = total
        own_parent[own * top : own * (top + 1), :] = rows[pl.ds(first, own), :]
    stream.wait(1 + 2 * top_dev)
    parents[...] = jnp.broadcast_to(own_parent[...].astype(BF16)[None], parents.shape)


def near_kernel(
    leaves, own, near_hbm, places_hbm, message, even_side, odd_side, early, blocks_hbm, kept, sent, sources,
    near_list, places, blocks, table, held, coef_table, coef_wide, listed, tabled, arrived,
):
    points = blocks.shape[4]
    rank = message.shape[1]
    span = leaves * own
    size = message.shape[0] - span
    each = size // leaves
    count = each // 2
    lists = Stream([(near_hbm, near_list), (places_hbm, places)], listed, 2)
    step = 4
    begin = early.shape[0]
    stream = Stream(
        [
            (blocks_hbm.at[pl.ds(leaf, step)], blocks.at[pl.ds(leaf - begin, step)])
            for leaf in range(begin, leaves, step)
        ],
        arrived,
        4,
    )
    me = lax.axis_index("leaf")
    order = ((even_side, 2 - 2 * (me % 2)), (message, 1), (odd_side, 2 * (me % 2)))
    tables = Stream(
        [
            (source.at[pl.ds(span, size)], table.at[pl.ds(pl.multiple_of(size * i, size), size)])
            for source, i in order
        ]
        + [
            (source.at[pl.ds(0, span)], coef_table.at[pl.ds(pl.multiple_of(span * i, span), span)])
            for source, i in order
        ],
        tabled,
        6,
    )
    first_leaf = me * leaves
    core = lax.axis_index("rhs") % 2
    for i in range(2):
        lists.wait(i)
    for i in range(6):
        tables.wait(i)
    for leaf in range(leaves):
        place = (near_list[0, leaf] - first_leaf + leaves) * each
        value = table[pl.ds(pl.multiple_of(place, each), each), :]
        held[leaf] = jnp.concatenate([value[:count], value[count:]], axis=1)
    coef_wide[...] = coef_table[...].astype(F32)
    for leaf in range(leaves):
        for slot in range(1, places.shape[0]):
            place = pl.multiple_of((places[slot, leaf] - first_leaf + leaves) * own, own)
            sources[own * leaf : own * (leaf + 1), rank * (slot - 1) : rank * slot] = coef_wide[
                pl.ds(place, own), :
            ]
    others = []
    for leaf in range(leaves):
        if leaf >= begin and leaf % step == 0:
            stream.wait((leaf - begin) // step)
        block = early[leaf, 0] if leaf < begin else blocks[leaf - begin, 0]
        product = dot(held[leaf], block.reshape(2 * points, points), ALONG_LAST)
        value = complex_rows(product)
        for part in range(2):
            row = 2 * own * leaf + own * part
            first = value[2 * own * part : 2 * own * part + own]
            second = value[2 * own * part + own : 2 * own * (part + 1)]
            kept[row : row + own, :] = jnp.where(core == 0, first, second)
            others.append(jnp.where(core == 0, second, first))
    sent[...] = jnp.concatenate(others).astype(BF16)


def coupling_kernel(leaves, own, distant, sources, coupling, field):
    rank = coupling.shape[4]
    for leaf in range(leaves):
        part = slice(own * leaf, own * (leaf + 1))
        value = jnp.concatenate([distant[part, :].astype(F32), sources[part, :]], axis=1)
        weights = jnp.concatenate(
            [coupling[leaf, slot].reshape(2 * rank, rank) for slot in range(coupling.shape[1])], axis=1
        )
        field[part, :] = complex_rows(dot(value.astype(BF16), weights, ALONG_LAST))


def sum_kernel(leaves, own, far, mine, received, product):
    for leaf in range(leaves):
        part = slice(own * leaf, own * (leaf + 1))
        value = far[part, :] + mine[part, :] + received[part, :].astype(F32)
        product[leaf] = value.astype(BF16).reshape(product.shape[1:])


def half_kernel(leaves, own, kept, received, mine, sent):
    part = lax.axis_index("rhs") // 2
    total = kept[...] + received[...].astype(F32)
    others = []
    for leaf in range(leaves):
        row = own * leaf
        first = total[2 * row : 2 * row + own]
        second = total[2 * row + own : 2 * row + 2 * own]
        mine[row : row + own, :] = jnp.where(part == 0, first, second)
        others.append(jnp.where(part == 0, second, first))
    sent[...] = jnp.concatenate(others).astype(BF16)


def down_kernel(
    leaves, own, tops_hbm, gathered, top_coupling, transfer, basis_hbm, field, result,
    tops, basis, table, listed, arrived,
):
    rank = transfer.shape[2]
    top_dev = top_coupling.shape[0]
    slots = top_coupling.shape[1]
    branch = leaves // top_dev
    lists = Stream([(tops_hbm, tops)], listed, 1)
    stream = Stream([(basis_hbm, basis)], arrived, 1)
    table[...] = gathered[...].astype(F32).reshape(table.shape)
    lists.wait(0)
    pairs = []
    for top in range(top_dev):
        values = []
        for slot in range(slots):
            values.append(table[pl.ds(pl.multiple_of(tops[top, slot] * own, own), own), :])
        value = jnp.concatenate(values, axis=1).astype(BF16)
        weights = jnp.concatenate(
            [top_coupling[top, slot].reshape(2 * rank, rank) for slot in range(slots)], axis=1
        )
        top_field = complex_rows(dot(value, weights, ALONG_LAST)).astype(BF16)
        for leaf in range(top * branch, (top + 1) * branch):
            down = complex_rows(dot(top_field, transfer[leaf].reshape(2 * rank, rank), ALONG_LAST))
            value = (down + field[own * leaf : own * (leaf + 1), :]).astype(BF16).astype(F32)
            pairs.append(jnp.concatenate([value, turned(value)], axis=1).astype(BF16))
    stream.wait(0)
    for leaf in range(leaves):
        result[own * leaf : own * (leaf + 1), :] = dot(
            pairs[leaf], basis[leaf].reshape(2 * rank, -1), ALONG_ROWS
        )


VMEM = pl.BlockSpec(memory_space=pltpu.VMEM)
SMEM = pl.BlockSpec(memory_space=pltpu.SMEM)
HBM = pl.BlockSpec(memory_space=pltpu.HBM)
ANY = pl.BlockSpec(memory_space=pl.ANY)


def call(kernel, out_shape, scratch, ops, specs, flops, room):
    ops = [
        pltpu.with_memory_space_constraint(value, pltpu.HBM) if specs.get(i) is HBM else value
        for i, value in enumerate(ops)
    ]
    return pl.pallas_call(
        kernel,
        out_shape=[jax.ShapeDtypeStruct(*shape) for shape in out_shape],
        in_specs=[specs.get(i, VMEM) for i in range(len(ops))],
        out_specs=[VMEM] * len(out_shape),
        scratch_shapes=scratch,
        compiler_params=pltpu.CompilerParams(vmem_limit_bytes=room * 2**20),
        cost_estimate=pl.CostEstimate(flops=flops, bytes_accessed=4 * 2**20, transcendentals=0),
    )(*ops)


def shifted(value, axis, step):
    count = lax.axis_size(axis)
    return lax.ppermute(value, axis, [(i, (i - step) % count) for i in range(count)])


def paired(value, axis, first):
    count = lax.axis_size(axis)
    pairs = []
    for i in range(first, count - 1, 2):
        pairs += [(i, i + 1), (i + 1, i)]
    return lax.ppermute(value, axis, pairs)


def flipped(value, axis, bit):
    count = lax.axis_size(axis)
    return lax.ppermute(value, axis, [(i, i ^ bit) for i in range(count)])


def local(
    charges,
    near_blocks,
    near_list,
    basis,
    coupling,
    coupling_list,
    transfer,
    top_coupling,
    top_list,
):
    leaves, rhs_all, _, points = charges.shape
    rhs_dev = rhs_all // lax.axis_size("rhs")
    top_dev = top_coupling.shape[0]
    rank = basis.shape[2]
    groups = lax.axis_size("leaf")
    count, own = 2 * rhs_all, 2 * rhs_dev
    parent_rows, coef_rows = top_dev * own, leaves * own
    parents, coefs, message, early = call(
        functools.partial(up_kernel, leaves, top_dev, own),
        [
            ((groups, parent_rows, rank), BF16),
            ((coef_rows, rank), BF16),
            ((coef_rows + leaves * 2 * count, rank), BF16),
            ((leaves // 2, *near_blocks.shape[1:]), BF16),
        ],
        [
            pltpu.VMEM(charges.shape, BF16),
            pltpu.VMEM(basis.shape, BF16),
            pltpu.VMEM(transfer.shape, BF16),
            pltpu.VMEM((leaves, count, points), BF16),
            pltpu.VMEM((leaves, count, rank), F32),
            pltpu.VMEM((count, rank), F32),
            pltpu.VMEM((coef_rows, rank), F32),
            pltpu.VMEM((parent_rows, rank), F32),
            pltpu.SemaphoreType.DMA((2 + 2 * top_dev,)),
        ],
        (charges, basis, transfer, near_blocks),
        {0: HBM, 1: HBM, 2: HBM, 3: HBM},
        2 * 10**8,
        12,
    )
    gathered = lax.all_to_all(parents, "leaf", 0, 0, tiled=True)
    odd_side = paired(message, "leaf", 1)
    even_side = paired(message, "leaf", 0)
    distant = shifted(coefs, "leaf", groups // 2)
    kept, sent, sources = call(
        functools.partial(near_kernel, leaves, own),
        [
            ((leaves * 2 * own, points), F32),
            ((leaves * 2 * own, points), BF16),
            ((coef_rows, 3 * rank), F32),
        ],
        [
            pltpu.SMEM((1, leaves), jnp.int32),
            pltpu.SMEM((coupling_list.shape[1], leaves), jnp.int32),
            pltpu.VMEM((leaves // 2, *near_blocks.shape[1:]), BF16),
            pltpu.VMEM((3 * leaves * 2 * count, rank), BF16),
            pltpu.VMEM((leaves, count, points), BF16),
            pltpu.VMEM((3 * coef_rows, rank), BF16),
            pltpu.VMEM((3 * coef_rows, rank), F32),
            pltpu.SemaphoreType.DMA((2,)),
            pltpu.SemaphoreType.DMA((6,)),
            pltpu.SemaphoreType.DMA((leaves // 8,)),
        ],
        (near_list.T, coupling_list.T, message, even_side, odd_side, early, near_blocks),
        {0: HBM, 1: HBM, 2: ANY, 3: ANY, 4: ANY, 6: HBM},
        2 * 10**9,
        8,
    )
    received = flipped(sent, "rhs", 1)
    mine, sent = call(
        functools.partial(half_kernel, leaves, own),
        [((leaves * own, points), F32), ((leaves * own, points), BF16)],
        [],
        (kept, received),
        {},
        2 * 10**9,
        2,
    )
    sources, mine = lax.optimization_barrier((sources, mine))
    received = flipped(sent, "rhs", 2)
    (field,) = call(
        functools.partial(coupling_kernel, leaves, own),
        [((coef_rows, rank), F32)],
        [],
        (distant, sources, coupling),
        {},
        2 * 10**9,
        6,
    )
    (far_part,) = call(
        functools.partial(down_kernel, leaves, own),
        [((leaves * own, points), F32)],
        [
            pltpu.SMEM(top_list.shape, jnp.int32),
            pltpu.VMEM(basis.shape, BF16),
            pltpu.VMEM((groups * parent_rows, rank), F32),
            pltpu.SemaphoreType.DMA((1,)),
            pltpu.SemaphoreType.DMA((1,)),
        ],
        (top_list, gathered, top_coupling, transfer, basis, field),
        {0: HBM, 4: HBM},
        2 * 10**9,
        6,
    )
    (product,) = call(
        functools.partial(sum_kernel, leaves, own),
        [((leaves, rhs_dev, 2, points), BF16)],
        [],
        (far_part, mine, received),
        {},
        10**7,
        2,
    )
    return product


def solution(mesh):
    return jax.shard_map(
        local,
        mesh=mesh,
        in_specs=(
            P("leaf", None, None, None),
            P("leaf", "rhs", None, None, None),
            P("leaf", "rhs"),
            P("leaf", None, None, None),
            P("leaf", None, None, None, None),
            P("leaf", None),
            P("leaf", None, None, None),
            P("leaf", None, None, None, None),
            P("leaf", None),
        ),
        out_specs=P("leaf", "rhs", None, None),
        check_vma=False,
    )
```

```python
import functools

import jax
import jax.numpy as jnp
from jax import lax
from jax.experimental import pallas as pl
from jax.experimental.pallas import tpu as pltpu
from jax.sharding import PartitionSpec as P

F32 = jnp.float32
BF16 = jnp.bfloat16
ALONG_LAST = (((1,), (1,)), ((), ()))
ALONG_ROWS = (((1,), (0,)), ((), ()))


def dot(left, right, dims):
    return lax.dot_general(left, right, dims, preferred_element_type=F32)


def turned(value):
    rows = value.shape[0]
    even = lax.broadcasted_iota(jnp.int32, value.shape, 0) % 2 == 0
    return jnp.where(even, -pltpu.roll(value, rows - 1, 0), pltpu.roll(value, 1, 0))


def complex_rows(value):
    half = value.shape[1] // 2
    return value[:, :half] + turned(value[:, half:])


class Stream:
    def __init__(self, pairs, arrived, ahead):
        self.copies = [
            pltpu.make_async_copy(source, target, arrived.at[i])
            for i, (source, target) in enumerate(pairs)
        ]
        self.ahead = ahead
        for copy in self.copies[:ahead]:
            copy.start()

    def wait(self, index):
        self.copies[index].wait()
        if index + self.ahead < len(self.copies):
            self.copies[index + self.ahead].start()


def up_kernel(
    leaves, top_dev, own, charges_hbm, basis_hbm, transfer_hbm, blocks_hbm, parents, coefs, message, early,
    charges, basis, transfer, held, coef, rows, own_coef, own_parent, arrived,
):
    rank = basis.shape[2]
    branch = leaves // top_dev
    parts = [pl.ds(top * branch, branch) for top in range(top_dev)]
    stream = Stream(
        [(charges_hbm, charges)]
        + [(basis_hbm.at[part], basis.at[part]) for part in parts]
        + [(transfer_hbm.at[part], transfer.at[part]) for part in parts]
        + [(blocks_hbm.at[pl.ds(0, early.shape[0])], early)],
        arrived,
        2 + 2 * top_dev,
    )
    count = charges.shape[1] * 2
    first = pl.multiple_of(lax.axis_index("rhs") * own, own)
    coef_rows = leaves * own
    stream.wait(0)
    for leaf in range(leaves):
        source = charges[leaf].reshape(count, charges.shape[3])
        held[leaf] = source
        start = coef_rows + 2 * count * leaf
        message[start : start + count, :] = source[:, :rank]
        message[start + count : start + 2 * count, :] = source[:, rank:]
    for leaf in range(leaves):
        if leaf % (2 * branch) == 0:
            stream.wait(1 + leaf // branch)
            stream.wait(2 + leaf // branch)
        product = dot(held[leaf], basis[leaf].reshape(2 * rank, -1), ALONG_LAST)
        coef[leaf] = complex_rows(product)
    for leaf in range(leaves):
        own_coef[own * leaf : own * (leaf + 1), :] = coef[leaf, pl.ds(first, own), :]
    coefs[...] = own_coef[...].astype(BF16)
    message[:coef_rows, :] = own_coef[...].astype(BF16)
    for top in range(top_dev):
        stream.wait(1 + top_dev + top)
    for top in range(top_dev):
        total = jnp.zeros((count, rank), F32)
        for leaf in range(top * branch, (top + 1) * branch):
            value = coef[leaf].astype(BF16).astype(F32)
            pair = jnp.concatenate([value, turned(value)], axis=1).astype(BF16)
            total += dot(pair, transfer[leaf].reshape(2 * rank, -1), ALONG_ROWS)
        rows[...] = total
        own_parent[own * top : own * (top + 1), :] = rows[pl.ds(first, own), :]
    stream.wait(1 + 2 * top_dev)
    parents[...] = jnp.broadcast_to(own_parent[...].astype(BF16)[None], parents.shape)


def near_kernel(
    leaves, own, near_hbm, places_hbm, message, even_side, odd_side, early, blocks_hbm, kept, sent, sources,
    near_list, places, blocks, table, held, coef_table, coef_wide, listed, tabled, arrived,
):
    points = blocks.shape[4]
    rank = message.shape[1]
    span = leaves * own
    size = message.shape[0] - span
    each = size // leaves
    count = each // 2
    step = 4
    begin = early.shape[0]
    stream = Stream(
        [
            (blocks_hbm.at[pl.ds(leaf, step)], blocks.at[pl.ds(leaf - begin, step)])
            for leaf in range(begin, leaves, step)
        ],
        arrived,
        4,
    )
    lists = Stream([(near_hbm, near_list), (places_hbm, places)], listed, 2)
    me = lax.axis_index("leaf")
    order = ((even_side, 2 - 2 * (me % 2)), (message, 1), (odd_side, 2 * (me % 2)))
    tables = Stream(
        [
            (source.at[pl.ds(span, size)], table.at[pl.ds(pl.multiple_of(size * i, size), size)])
            for source, i in order
        ]
        + [
            (source.at[pl.ds(0, span)], coef_table.at[pl.ds(pl.multiple_of(span * i, span), span)])
            for source, i in order
        ],
        tabled,
        6,
    )
    first_leaf = me * leaves
    core = lax.axis_index("rhs") % 2
    for i in range(2):
        lists.wait(i)
    for i in range(6):
        tables.wait(i)
    for leaf in range(leaves):
        place = (near_list[0, leaf] - first_leaf + leaves) * each
        value = table[pl.ds(pl.multiple_of(place, each), each), :]
        held[leaf] = jnp.concatenate([value[:count], value[count:]], axis=1)
    coef_wide[...] = coef_table[...].astype(F32)
    for leaf in range(leaves):
        for slot in range(1, places.shape[0]):
            place = pl.multiple_of((places[slot, leaf] - first_leaf + leaves) * own, own)
            sources[own * leaf : own * (leaf + 1), rank * (slot - 1) : rank * slot] = coef_wide[
                pl.ds(place, own), :
            ]
    others = []
    for leaf in range(leaves):
        if leaf >= begin and leaf % step == 0:
            stream.wait((leaf - begin) // step)
        block = early[leaf, 0] if leaf < begin else blocks[leaf - begin, 0]
        product = dot(held[leaf], block.reshape(2 * points, points), ALONG_LAST)
        value = complex_rows(product)
        for part in range(2):
            row = 2 * own * leaf + own * part
            first = value[2 * own * part : 2 * own * part + own]
            second = value[2 * own * part + own : 2 * own * (part + 1)]
            kept[row : row + own, :] = jnp.where(core == 0, first, second)
            others.append(jnp.where(core == 0, second, first))
    sent[...] = jnp.concatenate(others).astype(BF16)


def coupling_kernel(leaves, own, distant, sources, coupling, field):
    rank = coupling.shape[4]
    for leaf in range(leaves):
        part = slice(own * leaf, own * (leaf + 1))
        value = jnp.concatenate([distant[part, :].astype(F32), sources[part, :]], axis=1)
        weights = jnp.concatenate(
            [coupling[leaf, slot].reshape(2 * rank, rank) for slot in range(coupling.shape[1])], axis=1
        )
        field[part, :] = complex_rows(dot(value.astype(BF16), weights, ALONG_LAST))


def sum_kernel(leaves, own, far, mine, received, product):
    for leaf in range(leaves):
        part = slice(own * leaf, own * (leaf + 1))
        value = far[part, :] + mine[part, :] + received[part, :].astype(F32)
        product[leaf] = value.astype(BF16).reshape(product.shape[1:])


def half_kernel(leaves, own, kept, received, mine, sent):
    part = lax.axis_index("rhs") // 2
    total = kept[...] + received[...].astype(F32)
    others = []
    for leaf in range(leaves):
        row = own * leaf
        first = total[2 * row : 2 * row + own]
        second = total[2 * row + own : 2 * row + 2 * own]
        mine[row : row + own, :] = jnp.where(part == 0, first, second)
        others.append(jnp.where(part == 0, second, first))
    sent[...] = jnp.concatenate(others).astype(BF16)


def down_kernel(
    leaves, own, tops_hbm, gathered, top_coupling, transfer, basis_hbm, field, result,
    tops, basis, table, listed, arrived,
):
    rank = transfer.shape[2]
    top_dev = top_coupling.shape[0]
    slots = top_coupling.shape[1]
    branch = leaves // top_dev
    lists = Stream([(tops_hbm, tops)], listed, 1)
    stream = Stream([(basis_hbm, basis)], arrived, 1)
    table[...] = gathered[...].astype(F32).reshape(table.shape)
    lists.wait(0)
    pairs = []
    for top in range(top_dev):
        values = []
        for slot in range(slots):
            values.append(table[pl.ds(pl.multiple_of(tops[top, slot] * own, own), own), :])
        value = jnp.concatenate(values, axis=1).astype(BF16)
        weights = jnp.concatenate(
            [top_coupling[top, slot].reshape(2 * rank, rank) for slot in range(slots)], axis=1
        )
        top_field = complex_rows(dot(value, weights, ALONG_LAST)).astype(BF16)
        for leaf in range(top * branch, (top + 1) * branch):
            down = complex_rows(dot(top_field, transfer[leaf].reshape(2 * rank, rank), ALONG_LAST))
            value = (down + field[own * leaf : own * (leaf + 1), :]).astype(BF16).astype(F32)
            pairs.append(jnp.concatenate([value, turned(value)], axis=1).astype(BF16))
    stream.wait(0)
    for leaf in range(leaves):
        result[own * leaf : own * (leaf + 1), :] = dot(
            pairs[leaf], basis[leaf].reshape(2 * rank, -1), ALONG_ROWS
        )


VMEM = pl.BlockSpec(memory_space=pltpu.VMEM)
SMEM = pl.BlockSpec(memory_space=pltpu.SMEM)
HBM = pl.BlockSpec(memory_space=pltpu.HBM)
ANY = pl.BlockSpec(memory_space=pl.ANY)


def call(kernel, out_shape, scratch, ops, specs, flops, room):
    ops = [
        pltpu.with_memory_space_constraint(value, pltpu.HBM) if specs.get(i) is HBM else value
        for i, value in enumerate(ops)
    ]
    return pl.pallas_call(
        kernel,
        out_shape=[jax.ShapeDtypeStruct(*shape) for shape in out_shape],
        in_specs=[specs.get(i, VMEM) for i in range(len(ops))],
        out_specs=[VMEM] * len(out_shape),
        scratch_shapes=scratch,
        compiler_params=pltpu.CompilerParams(vmem_limit_bytes=room * 2**20),
        cost_estimate=pl.CostEstimate(flops=flops, bytes_accessed=4 * 2**20, transcendentals=0),
    )(*ops)


def shifted(value, axis, step):
    count = lax.axis_size(axis)
    return lax.ppermute(value, axis, [(i, (i - step) % count) for i in range(count)])


def paired(value, axis, first):
    count = lax.axis_size(axis)
    pairs = []
    for i in range(first, count - 1, 2):
        pairs += [(i, i + 1), (i + 1, i)]
    return lax.ppermute(value, axis, pairs)


def flipped(value, axis, bit):
    count = lax.axis_size(axis)
    return lax.ppermute(value, axis, [(i, i ^ bit) for i in range(count)])


def local(
    charges,
    near_blocks,
    near_list,
    basis,
    coupling,
    coupling_list,
    transfer,
    top_coupling,
    top_list,
):
    leaves, rhs_all, _, points = charges.shape
    rhs_dev = rhs_all // lax.axis_size("rhs")
    top_dev = top_coupling.shape[0]
    rank = basis.shape[2]
    groups = lax.axis_size("leaf")
    count, own = 2 * rhs_all, 2 * rhs_dev
    parent_rows, coef_rows = top_dev * own, leaves * own
    parents, coefs, message, early = call(
        functools.partial(up_kernel, leaves, top_dev, own),
        [
            ((groups, parent_rows, rank), BF16),
            ((coef_rows, rank), BF16),
            ((coef_rows + leaves * 2 * count, rank), BF16),
            ((leaves // 2, *near_blocks.shape[1:]), BF16),
        ],
        [
            pltpu.VMEM(charges.shape, BF16),
            pltpu.VMEM(basis.shape, BF16),
            pltpu.VMEM(transfer.shape, BF16),
            pltpu.VMEM((leaves, count, points), BF16),
            pltpu.VMEM((leaves, count, rank), F32),
            pltpu.VMEM((count, rank), F32),
            pltpu.VMEM((coef_rows, rank), F32),
            pltpu.VMEM((parent_rows, rank), F32),
            pltpu.SemaphoreType.DMA((2 + 2 * top_dev,)),
        ],
        (charges, basis, transfer, near_blocks),
        {0: HBM, 1: HBM, 2: HBM, 3: HBM},
        2 * 10**8,
        12,
    )
    gathered = lax.all_to_all(parents, "leaf", 0, 0, tiled=True)
    odd_side = paired(message, "leaf", 1)
    even_side = paired(message, "leaf", 0)
    distant = shifted(coefs, "leaf", groups // 2)
    kept, sent, sources = call(
        functools.partial(near_kernel, leaves, own),
        [
            ((leaves * 2 * own, points), F32),
            ((leaves * 2 * own, points), BF16),
            ((coef_rows, 3 * rank), F32),
        ],
        [
            pltpu.SMEM((1, leaves), jnp.int32),
            pltpu.SMEM((coupling_list.shape[1], leaves), jnp.int32),
            pltpu.VMEM((leaves // 2, *near_blocks.shape[1:]), BF16),
            pltpu.VMEM((3 * leaves * 2 * count, rank), BF16),
            pltpu.VMEM((leaves, count, points), BF16),
            pltpu.VMEM((3 * coef_rows, rank), BF16),
            pltpu.VMEM((3 * coef_rows, rank), F32),
            pltpu.SemaphoreType.DMA((2,)),
            pltpu.SemaphoreType.DMA((6,)),
            pltpu.SemaphoreType.DMA((leaves // 8,)),
        ],
        (near_list.T, coupling_list.T, message, even_side, odd_side, early, near_blocks),
        {0: HBM, 1: HBM, 2: ANY, 3: ANY, 4: ANY, 6: HBM},
        2 * 10**9,
        8,
    )
    received = flipped(sent, "rhs", 1)
    mine, sent = call(
        functools.partial(half_kernel, leaves, own),
        [((leaves * own, points), F32), ((leaves * own, points), BF16)],
        [],
        (kept, received),
        {},
        2 * 10**9,
        2,
    )
    sources, mine = lax.optimization_barrier((sources, mine))
    received = flipped(sent, "rhs", 2)
    (field,) = call(
        functools.partial(coupling_kernel, leaves, own),
        [((coef_rows, rank), F32)],
        [],
        (distant, sources, coupling),
        {},
        2 * 10**9,
        6,
    )
    (far_part,) = call(
        functools.partial(down_kernel, leaves, own),
        [((leaves * own, points), F32)],
        [
            pltpu.SMEM(top_list.shape, jnp.int32),
            pltpu.VMEM(basis.shape, BF16),
            pltpu.VMEM((groups * parent_rows, rank), F32),
            pltpu.SemaphoreType.DMA((1,)),
            pltpu.SemaphoreType.DMA((1,)),
        ],
        (top_list, gathered, top_coupling, transfer, basis, field),
        {0: HBM, 4: HBM},
        2 * 10**9,
        6,
    )
    (product,) = call(
        functools.partial(sum_kernel, leaves, own),
        [((leaves, rhs_dev, 2, points), BF16)],
        [],
        (far_part, mine, received),
        {},
        10**7,
        2,
    )
    return product


def solution(mesh):
    return jax.shard_map(
        local,
        mesh=mesh,
        in_specs=(
            P("leaf", None, None, None),
            P("leaf", "rhs", None, None, None),
            P("leaf", "rhs"),
            P("leaf", None, None, None),
            P("leaf", None, None, None, None),
            P("leaf", None),
            P("leaf", None, None, None),
            P("leaf", None, None, None, None),
            P("leaf", None),
        ),
        out_specs=P("leaf", "rhs", None, None),
        check_vma=False,
    )
```
